32 devices in a mesh: groups: 1, shard: 16 (over z, y, core), layer: 2 (over x).
Axes of the slice: x: 2, y: 2, z: 4, core: 2. Of those that a mesh axis runs over, the one named last changes fastest.
Arguments:
- train_grads: bfloat16 [8192, 2, 4096], P(('groups', 'shard'), 'layer'), may hold values from -0.049804688 to 0.049804688
- queries: bfloat16 [256, 2, 4096], P('shard', 'layer'), may hold values from -6 to 6
- basis_in: float32 [2, 64, 64], P('layer'), may hold values from -0.75 to 0.75
- basis_out: float32 [2, 64, 64], P('layer'), may hold values from -0.75 to 0.75
- eigen: float32 [2, 64, 64], P('layer'), may hold values from 0.05 to 5
Outputs:
- scores: float32 [8192, 256], P(('groups', 'shard'), 'layer')
The draws below stay inside these ranges and needn't reach their ends.
All inputs are finite; a program needn't handle non-finite values.
Results may differ from the reference program's by a relative error of at most 0.0029.
Values may be sent and summed in bfloat16 or wider, within the bound.
A program may use at most 64 MiB of HBM per device.

```python
import math
import jax
import jax.numpy as jnp
from jax import lax

R = 64
LAYERS = 2
NTRAIN = 8192
NQ = 256


def block_scale(key, dims, cuts, low, top_value):
    gain, own = 1.0, jax.random.fold_in(key, 6)
    for axis_at, blocks in cuts:
        steps = jnp.exp(jax.random.uniform(jax.random.fold_in(own, axis_at), (blocks,), jnp.float32, low / len(cuts), top_value / len(cuts)))
        gain = gain * jnp.repeat(steps, dims[axis_at] // blocks).reshape([-1 if axis == axis_at else 1 for axis in range(len(dims))])
    return gain


def scatter_about(key, extent, width, limit, split=(), held_as=jnp.bfloat16):
    loudness = block_scale(key, extent, split, -0.22, 0.18) if split else 1.0
    drawn = jax.random.normal(key, extent, jnp.float32) * width * loudness
    return jnp.minimum(jnp.maximum(drawn, -limit), limit).astype(held_as)


def setup_inputs(seed: int = 0, part: int = 0) -> dict:
    streams_of = jax.random.split(jax.random.key(seed), 6)
    part_splits = jax.random.split(jax.random.fold_in(streams_of[5], part), 6)
    train_grads = scatter_about(part_splits[0], (NTRAIN, LAYERS, R * R), 0.0078125, 0.049804688, ((0, 16), (1, 2)))
    queries = scatter_about(streams_of[1], (NQ, LAYERS, R * R), 1.0, 6.0, ((0, 16), (1, 2)))
    basis_in = scatter_about(streams_of[2], (LAYERS, R, R), R ** -0.5, 0.75, ((0, 2),), jnp.float32)
    basis_out = scatter_about(streams_of[3], (LAYERS, R, R), R ** -0.5, 0.75, ((0, 2),), jnp.float32)
    eigen = jnp.clip(jnp.exp(math.log(5.0) - 4.6051702 * jax.random.uniform(streams_of[4], (LAYERS, R, R), jnp.float32) ** block_scale(streams_of[4], (LAYERS, R, R), ((0, 2),), -0.2, 0.2)), 0.05, 5.0)
    return dict(train_grads=train_grads, queries=queries, basis_in=basis_in, basis_out=basis_out, eigen=eigen)


def precondition(queries, basis_in, basis_out, eigen):
    count = queries.shape[0]
    layers = queries.shape[1]
    side = basis_in.shape[-1]
    grads = queries.astype(jnp.float32).reshape(count, layers, side, side)
    hp = lax.Precision.HIGHEST
    rotated = jnp.einsum("lai,qlab,lbj->qlij", basis_out, grads, basis_in, precision=hp)
    scaled = rotated / (eigen + 0.1)
    result = jnp.einsum("lia,qlab,ljb->qlij", basis_out, scaled, basis_in, precision=hp)
    return result.reshape(count, layers, side * side).astype(jnp.bfloat16)


def reference(train_grads, queries, basis_in, basis_out, eigen):
    precond = precondition(queries, basis_in, basis_out, eigen)
    total = jnp.zeros((train_grads.shape[0], queries.shape[0]), jnp.float32)
    for index in range(LAYERS):
        total = total + lax.dot_general(train_grads[:, index, :], precond[:, index, :], (((1,), (1,)), ((), ())), preferred_element_type=jnp.float32)
    return total
```

```python
import functools

import jax
import jax.numpy as jnp
from jax import lax
from jax.experimental import pallas as pl
from jax.experimental.pallas import tpu as pltpu
from jax.sharding import PartitionSpec as P

MESH = pl.DeviceIdType.MESH


def precondition(queries, basis_in, basis_out, eigen):
    count = queries.shape[0]
    layers = queries.shape[1]
    side = basis_in.shape[-1]
    grads = queries.astype(jnp.float32).reshape(count, layers, side, side)
    highest = lax.Precision.HIGHEST
    rotated = jnp.einsum("lai,qlab,lbj->qlij", basis_out, grads, basis_in, precision=highest)
    scaled = rotated / (eigen + 0.1)
    result = jnp.einsum("lia,qlab,ljb->qlij", basis_out, scaled, basis_in, precision=highest)
    return result.reshape(count, layers * side * side).astype(jnp.bfloat16)


def score_block(left, right):
    return lax.dot_general(
        left, right, (((1,), (1,)), ((), ())), preferred_element_type=jnp.float32
    )


def kernel(depth, p_ref, t_hbm, o_ref, buf, train, own, outgoing, incoming,
           load_sem, recv, send_right, send_left, send_y, send_core, recv_x, send_x):
    me = lax.axis_index("shard")
    layer = lax.axis_index("layer")
    core = lax.rem(me, 2)
    y = lax.rem(me // 2, 2)
    z = me // 4
    half = depth // 2
    mine = y * 2 + core
    across = (1 - y) * 2 + core
    sibling = y * 2 + (1 - core)
    diagonal = (1 - y) * 2 + (1 - core)

    load = pltpu.make_async_copy(t_hbm, train, load_sem)
    load.start()

    barrier = pltpu.get_barrier_semaphore()
    pl.semaphore_signal(barrier, inc=1, device_id={"shard": z * 4 + across}, device_id_type=MESH)
    pl.semaphore_signal(barrier, inc=1, device_id={"shard": z * 4 + sibling}, device_id_type=MESH)
    pl.semaphore_signal(barrier, inc=1, device_id={"layer": 1 - layer}, device_id_type=MESH)

    @pl.when(z > 0)
    def _():
        pl.semaphore_signal(barrier, inc=1, device_id={"shard": me - 4}, device_id_type=MESH)

    @pl.when(z < depth - 1)
    def _():
        pl.semaphore_signal(barrier, inc=1, device_id={"shard": me + 4}, device_id_type=MESH)

    buf[z, mine] = p_ref[...]
    pl.semaphore_wait(barrier, 3 + jnp.where(z > 0, 1, 0) + jnp.where(z < depth - 1, 1, 0))

    def chunk(column, row, device, sem):
        return pltpu.make_async_remote_copy(
            src_ref=buf.at[column, row],
            dst_ref=buf.at[column, row],
            send_sem=sem,
            recv_sem=recv.at[column, row],
            device_id={"shard": device},
            device_id_type=MESH,
        )

    def to_right(column):
        return chunk(column, mine, me + 4, send_right.at[column])

    def to_left(column):
        return chunk(column, mine, me - 4, send_left.at[column])

    def to_y(column):
        return chunk(column, mine, z * 4 + across, send_y.at[column])

    def to_core(column, row):
        return chunk(column, row, z * 4 + sibling, send_core.at[column, row])

    def arrived(column, row):
        chunk(column, row, z * 4 + sibling, send_core.at[column, row]).wait_recv()

    def partial_copy(slot):
        return pltpu.make_async_remote_copy(
            src_ref=outgoing.at[slot],
            dst_ref=incoming.at[slot],
            send_sem=send_x.at[slot],
            recv_sem=recv_x.at[slot],
            device_id={"layer": 1 - layer},
            device_id_type=MESH,
        )

    def spread(column):
        to_y(column).start()
        to_core(column, mine).start()

    def finish(column):
        arrived(column, across)
        to_core(column, across).start()
        arrived(column, sibling)
        arrived(column, diagonal)
        block = score_block(buf[column].reshape(-1, buf.shape[-1]), train[...])
        slot = lax.rem(column, half)
        kept = column // half == layer

        @pl.when(kept)
        def _():
            own[slot] = block

        @pl.when(jnp.logical_not(kept))
        def _():
            outgoing[slot] = block.astype(outgoing.dtype)
            partial_copy(slot).start()

    @pl.when(z < depth - 1)
    def _():
        to_right(z).start()

    @pl.when(z > 0)
    def _():
        to_left(z).start()

    spread(z)

    for step in range(1, depth):
        @pl.when(z >= step)
        def _():
            column = z - step
            arrived(column, mine)

            @pl.when(z < depth - 1)
            def _():
                to_right(column).start()

            spread(column)

        @pl.when(z + step < depth)
        def _():
            column = z + step
            arrived(column, mine)

            @pl.when(z > 0)
            def _():
                to_left(column).start()

            spread(column)

        if step == 1:
            load.wait()
            finish(z)
        else:
            back = step - 1

            @pl.when(z >= back)
            def _():
                finish(z - back)

            @pl.when(z + back < depth)
            def _():
                finish(z + back)

    back = depth - 1

    @pl.when(z >= back)
    def _():
        finish(z - back)

    @pl.when(z + back < depth)
    def _():
        finish(z + back)

    for slot in range(half):
        partial_copy(slot).wait_recv()
        total = own[slot] + incoming[slot].astype(jnp.float32)
        own[slot] = total
    o_ref[...] = own[...].reshape(-1, own.shape[-1]).T

    for slot in range(half):
        partial_copy(slot).wait_send()
    for column in range(depth):
        to_y(column).wait_send()
        to_core(column, mine).wait_send()
        to_core(column, across).wait_send()

        @pl.when(jnp.logical_and(z >= column, z < depth - 1))
        def _():
            to_right(column).wait_send()

        @pl.when(jnp.logical_and(z <= column, z > 0))
        def _():
            to_left(column).wait_send()


def fused_scores(precond, train_flat, shards):
    count, width = precond.shape
    examples = train_flat.shape[0]
    depth = shards // 4
    half = depth // 2
    dma = pltpu.SemaphoreType.DMA
    return pl.pallas_call(
        functools.partial(kernel, depth),
        out_shape=jax.ShapeDtypeStruct((examples, half * 4 * count), jnp.float32),
        in_specs=[
            pl.BlockSpec(memory_space=pltpu.VMEM),
            pl.BlockSpec(memory_space=pl.ANY),
        ],
        out_specs=pl.BlockSpec(memory_space=pltpu.VMEM),
        scratch_shapes=[
            pltpu.VMEM((depth, 4, count, width), jnp.bfloat16),
            pltpu.VMEM((examples, width), jnp.bfloat16),
            pltpu.VMEM((half, 4 * count, examples), jnp.float32),
            pltpu.VMEM((half, 4 * count, examples), jnp.bfloat16),
            pltpu.VMEM((half, 4 * count, examples), jnp.bfloat16),
            dma,
            dma((depth, 4)),
            dma((depth,)),
            dma((depth,)),
            dma((depth,)),
            dma((depth, 4)),
            dma((half,)),
            dma((half,)),
        ],
        compiler_params=pltpu.CompilerParams(
            collective_id=0, has_side_effects=True, vmem_limit_bytes=48 * 1024 * 1024
        ),
    )(precond, train_flat)


def body(fused, shards, train_grads, queries, basis_in, basis_out, eigen):
    examples = train_grads.shape[0]
    train_flat = train_grads.reshape(examples, train_grads.shape[1] * train_grads.shape[2])
    precond = precondition(queries, basis_in, basis_out, eigen)
    if fused:
        return fused_scores(precond, train_flat, shards)
    gathered = lax.all_gather(precond, "shard", axis=0, tiled=True)
    mine = lax.psum_scatter(
        score_block(gathered, train_flat), "layer", scatter_dimension=0, tiled=True
    )
    return jnp.transpose(mine)


def solution(mesh):
    placed = (
        P(("groups", "shard"), "layer", None),
        P("shard", "layer", None),
        P("layer", None, None),
        P("layer", None, None),
        P("layer", None, None),
    )
    shards = mesh.shape["shard"]
    fused = mesh.shape["groups"] == 1 and mesh.shape["layer"] == 2 and shards == 16
    return jax.shard_map(
        functools.partial(body, fused, shards), mesh=mesh, in_specs=placed,
        out_specs=P(("groups", "shard"), "layer"), check_vma=False
    )
```

```python
import functools

import jax
import jax.numpy as jnp
from jax import lax
from jax.experimental import pallas as pl
from jax.experimental.pallas import tpu as pltpu
from jax.sharding import PartitionSpec as P

MESH = pl.DeviceIdType.MESH


def precondition(queries, basis_in, basis_out, eigen):
    count = queries.shape[0]
    layers = queries.shape[1]
    side = basis_in.shape[-1]
    grads = queries.astype(jnp.float32).reshape(count, layers, side, side)
    highest = lax.Precision.HIGHEST
    rotated = jnp.einsum("lai,qlab,lbj->qlij", basis_out, grads, basis_in, precision=highest)
    scaled = rotated / (eigen + 0.1)
    result = jnp.einsum("lia,qlab,ljb->qlij", basis_out, scaled, basis_in, precision=highest)
    return result.reshape(count, layers * side * side).astype(jnp.bfloat16)


def score_block(left, right):
    return lax.dot_general(
        left, right, (((1,), (1,)), ((), ())), preferred_element_type=jnp.float32
    )


def split(value):
    high = value.astype(jnp.bfloat16)
    return high, (value - high.astype(jnp.float32)).astype(jnp.bfloat16)


def dot(left, right):
    return jnp.dot(left, right, preferred_element_type=jnp.float32)


def twice_diagonal(block):
    empty = jnp.zeros_like(block)
    return jnp.concatenate(
        [jnp.concatenate([block, empty], 1), jnp.concatenate([empty, block], 1)], 0
    )


def swap_halves(value, side):
    return pltpu.roll(value, side, 1)


def precondition_block(q_ref, basis_in_ref, basis_out_ref, eigen_ref, rows_ref, store):
    count = q_ref.shape[0]
    side = basis_in_ref.shape[-1]
    lanes = 2 * side
    tiles = side // 2
    lower = lax.broadcasted_iota(jnp.int32, (tiles, lanes), 1) < side

    basis_in = basis_in_ref[...]
    in_high, in_low = split(twice_diagonal(basis_in))
    back_high, back_low = split(twice_diagonal(basis_in.T))
    ordered = jnp.concatenate(
        [basis_out_ref[pl.ds(0, tiles, stride=2), :], basis_out_ref[pl.ds(1, tiles, stride=2), :]], 0
    )
    out_high, out_low = split(ordered)
    turn_high, turn_low = split(ordered.T)
    inverse = 1.0 / (eigen_ref[...] + 0.1)
    inverse = jnp.concatenate([inverse, inverse], 1)

    stacked = jnp.concatenate(
        [q_ref[:, t * lanes:(t + 1) * lanes] for t in range(tiles)], 0
    )
    both = dot(stacked, jnp.concatenate([in_high, in_low], 1))
    rows_ref[...] = both[:, :lanes] + both[:, lanes:]

    pairs = []
    for pair in range(count // 2):
        first = rows_ref[pl.ds(2 * pair, tiles, stride=count), :]
        second = rows_ref[pl.ds(2 * pair + 1, tiles, stride=count), :]
        even = jnp.where(lower, first, swap_halves(second, side))
        odd = jnp.where(lower, swap_halves(first, side), second)
        pairs.append(jnp.concatenate([even, odd], 0))
    high, low = split(jnp.concatenate(pairs, 1))
    rotated = dot(
        jnp.concatenate([turn_high, turn_high, turn_low], 1), jnp.concatenate([high, low, high], 0)
    )
    scaled = rotated * jnp.concatenate([inverse] * (count // 2), 1)
    high, low = split(scaled)
    lifted = dot(
        jnp.concatenate([out_high, out_high, out_low], 1), jnp.concatenate([high, low, high], 0)
    )
    queries = []
    for pair in range(count // 2):
        even = lifted[:tiles, pair * lanes:(pair + 1) * lanes]
        odd = lifted[tiles:, pair * lanes:(pair + 1) * lanes]
        queries.append(jnp.where(lower, even, swap_halves(odd, side)))
        queries.append(jnp.where(lower, swap_halves(even, side), odd))
    high, low = split(jnp.concatenate(queries, 0))
    both = dot(
        jnp.concatenate([high, low], 1),
        jnp.concatenate(
            [
                jnp.concatenate([back_high, back_low], 1),
                jnp.concatenate([back_high, jnp.zeros_like(back_low)], 1),
            ],
            0,
        ),
    )
    rows_ref[...] = both[:, :lanes] + both[:, lanes:]
    for t in range(tiles):
        store(t, rows_ref[pl.ds(t, count, stride=tiles), :].astype(jnp.bfloat16))


def kernel(depth, q_hbm, basis_in_hbm, basis_out_hbm, eigen_hbm, t_hbm, o_ref,
           queries, basis_in, basis_out, eigen, rows, buf, train, own, outgoing, incoming,
           load_sem, recv, send_right, send_left, send_y, send_core, recv_x, send_x):
    me = lax.axis_index("shard")
    layer = lax.axis_index("layer")
    core = lax.rem(me, 2)
    y = lax.rem(me // 2, 2)
    z = me // 4
    half = depth // 2
    mine = y * 2 + core
    across = (1 - y) * 2 + core
    sibling = y * 2 + (1 - core)
    diagonal = (1 - y) * 2 + (1 - core)

    smalls = [
        pltpu.make_async_copy(source, target, load_sem.at[index])
        for index, (source, target) in enumerate(
            [(q_hbm, queries), (basis_in_hbm, basis_in), (basis_out_hbm, basis_out), (eigen_hbm, eigen)]
        )
    ]
    for small in smalls:
        small.start()
    load = pltpu.make_async_copy(t_hbm, train, load_sem.at[len(smalls)])
    load.start()

    barrier = pltpu.get_barrier_semaphore()
    pl.semaphore_signal(barrier, inc=1, device_id={"shard": z * 4 + across}, device_id_type=MESH)
    pl.semaphore_signal(barrier, inc=1, device_id={"shard": z * 4 + sibling}, device_id_type=MESH)
    pl.semaphore_signal(barrier, inc=1, device_id={"layer": 1 - layer}, device_id_type=MESH)

    @pl.when(z > 0)
    def _():
        pl.semaphore_signal(barrier, inc=1, device_id={"shard": me - 4}, device_id_type=MESH)

    @pl.when(z < depth - 1)
    def _():
        pl.semaphore_signal(barrier, inc=1, device_id={"shard": me + 4}, device_id_type=MESH)

    for small in smalls:
        small.wait()

    def store(tile, value):
        buf[z, mine, :, tile * value.shape[1]:(tile + 1) * value.shape[1]] = value

    precondition_block(queries, basis_in, basis_out, eigen, rows, store)
    pl.semaphore_wait(barrier, 3 + jnp.where(z > 0, 1, 0) + jnp.where(z < depth - 1, 1, 0))

    def chunk(column, row, device, sem):
        return pltpu.make_async_remote_copy(
            src_ref=buf.at[column, row],
            dst_ref=buf.at[column, row],
            send_sem=sem,
            recv_sem=recv.at[column, row],
            device_id={"shard": device},
            device_id_type=MESH,
        )

    def to_right(column):
        return chunk(column, mine, me + 4, send_right.at[column])

    def to_left(column):
        return chunk(column, mine, me - 4, send_left.at[column])

    def to_y(column):
        return chunk(column, mine, z * 4 + across, send_y.at[column])

    def to_core(column, row):
        return chunk(column, row, z * 4 + sibling, send_core.at[column, row])

    def arrived(column, row):
        chunk(column, row, z * 4 + sibling, send_core.at[column, row]).wait_recv()

    def partial_copy(slot):
        return pltpu.make_async_remote_copy(
            src_ref=outgoing.at[slot],
            dst_ref=incoming.at[slot],
            send_sem=send_x.at[slot],
            recv_sem=recv_x.at[slot],
            device_id={"layer": 1 - layer},
            device_id_type=MESH,
        )

    def spread(column):
        to_y(column).start()
        to_core(column, mine).start()

    def finish(column):
        arrived(column, across)
        to_core(column, across).start()
        arrived(column, sibling)
        arrived(column, diagonal)
        block = score_block(buf[column].reshape(-1, buf.shape[-1]), train[...])
        slot = lax.rem(column, half)
        kept = column // half == layer

        @pl.when(kept)
        def _():
            own[slot] = block

        @pl.when(jnp.logical_not(kept))
        def _():
            outgoing[slot] = block.astype(outgoing.dtype)
            partial_copy(slot).start()

    @pl.when(z < depth - 1)
    def _():
        to_right(z).start()

    @pl.when(z > 0)
    def _():
        to_left(z).start()

    spread(z)

    for step in range(1, depth):
        @pl.when(z >= step)
        def _():
            column = z - step
            arrived(column, mine)

            @pl.when(z < depth - 1)
            def _():
                to_right(column).start()

            spread(column)

        @pl.when(z + step < depth)
        def _():
            column = z + step
            arrived(column, mine)

            @pl.when(z > 0)
            def _():
                to_left(column).start()

            spread(column)

        if step == 1:
            load.wait()
            finish(z)
        else:
            back = step - 1

            @pl.when(z >= back)
            def _():
                finish(z - back)

            @pl.when(z + back < depth)
            def _():
                finish(z + back)

    back = depth - 1

    @pl.when(z >= back)
    def _():
        finish(z - back)

    @pl.when(z + back < depth)
    def _():
        finish(z + back)

    for slot in range(half):
        partial_copy(slot).wait_recv()
        total = own[slot] + incoming[slot].astype(jnp.float32)
        own[slot] = total
    o_ref[...] = own[...].reshape(-1, own.shape[-1]).T

    for slot in range(half):
        partial_copy(slot).wait_send()
    for column in range(depth):
        to_y(column).wait_send()
        to_core(column, mine).wait_send()
        to_core(column, across).wait_send()

        @pl.when(jnp.logical_and(z >= column, z < depth - 1))
        def _():
            to_right(column).wait_send()

        @pl.when(jnp.logical_and(z <= column, z > 0))
        def _():
            to_left(column).wait_send()


def fused_scores(queries, basis_in, basis_out, eigen, train_flat, shards):
    count, width = queries.shape
    side = basis_in.shape[-1]
    examples = train_flat.shape[0]
    depth = shards // 4
    half = depth // 2
    dma = pltpu.SemaphoreType.DMA
    return pl.pallas_call(
        functools.partial(kernel, depth),
        out_shape=jax.ShapeDtypeStruct((examples, half * 4 * count), jnp.float32),
        in_specs=[pl.BlockSpec(memory_space=pl.ANY)] * 5,
        out_specs=pl.BlockSpec(memory_space=pltpu.VMEM),
        scratch_shapes=[
            pltpu.VMEM((count, width), jnp.bfloat16),
            pltpu.VMEM((side, side), jnp.float32),
            pltpu.VMEM((side, side), jnp.float32),
            pltpu.VMEM((side, side), jnp.float32),
            pltpu.VMEM((count * side // 2, 2 * side), jnp.float32),
            pltpu.VMEM((depth, 4, count, width), jnp.bfloat16),
            pltpu.VMEM((examples, width), jnp.bfloat16),
            pltpu.VMEM((half, 4 * count, examples), jnp.float32),
            pltpu.VMEM((half, 4 * count, examples), jnp.bfloat16),
            pltpu.VMEM((half, 4 * count, examples), jnp.bfloat16),
            dma((5,)),
            dma((depth, 4)),
            dma((depth,)),
            dma((depth,)),
            dma((depth,)),
            dma((depth, 4)),
            dma((half,)),
            dma((half,)),
        ],
        compiler_params=pltpu.CompilerParams(
            collective_id=0, has_side_effects=True, vmem_limit_bytes=60 * 1024 * 1024
        ),
    )(queries, basis_in, basis_out, eigen, train_flat)


def body(fused, shards, train_grads, queries, basis_in, basis_out, eigen):
    examples = train_grads.shape[0]
    train_flat = train_grads.reshape(examples, train_grads.shape[1] * train_grads.shape[2])
    if fused:
        return fused_scores(
            queries.reshape(queries.shape[0], -1), basis_in[0], basis_out[0], eigen[0], train_flat, shards
        )
    precond = precondition(queries, basis_in, basis_out, eigen)
    gathered = lax.all_gather(precond, "shard", axis=0, tiled=True)
    mine = lax.psum_scatter(
        score_block(gathered, train_flat), "layer", scatter_dimension=0, tiled=True
    )
    return jnp.transpose(mine)


def solution(mesh):
    placed = (
        P(("groups", "shard"), "layer", None),
        P("shard", "layer", None),
        P("layer", None, None),
        P("layer", None, None),
        P("layer", None, None),
    )
    shards = mesh.shape["shard"]
    fused = mesh.shape["groups"] == 1 and mesh.shape["layer"] == 2 and shards == 16
    return jax.shard_map(
        functools.partial(body, fused, shards), mesh=mesh, in_specs=placed,
        out_specs=P(("groups", "shard"), "layer"), check_vma=False
    )
```

```python
import functools

import jax
import jax.numpy as jnp
from jax import lax
from jax.experimental import pallas as pl
from jax.experimental.pallas import tpu as pltpu
from jax.sharding import PartitionSpec as P

MESH = pl.DeviceIdType.MESH
PIECES = 2


def precondition(queries, basis_in, basis_out, eigen):
    count = queries.shape[0]
    layers = queries.shape[1]
    side = basis_in.shape[-1]
    grads = queries.astype(jnp.float32).reshape(count, layers, side, side)
    highest = lax.Precision.HIGHEST
    rotated = jnp.einsum("lai,qlab,lbj->qlij", basis_out, grads, basis_in, precision=highest)
    scaled = rotated / (eigen + 0.1)
    result = jnp.einsum("lia,qlab,ljb->qlij", basis_out, scaled, basis_in, precision=highest)
    return result.reshape(count, layers * side * side).astype(jnp.bfloat16)


def score_block(left, right):
    return lax.dot_general(
        left, right, (((1,), (1,)), ((), ())), preferred_element_type=jnp.float32
    )


def split(value):
    high = value.astype(jnp.bfloat16)
    return high, (value - high.astype(jnp.float32)).astype(jnp.bfloat16)


def dot(left, right):
    return jnp.dot(left, right, preferred_element_type=jnp.float32)


def twice_diagonal(block):
    empty = jnp.zeros_like(block)
    return jnp.concatenate(
        [jnp.concatenate([block, empty], 1), jnp.concatenate([empty, block], 1)], 0
    )


def swap_halves(value, side):
    return pltpu.roll(value, side, 1)


def precondition_block(q_ref, basis_in_ref, basis_out_ref, eigen_ref, rows_ref, store):
    count = q_ref.shape[0]
    side = basis_in_ref.shape[-1]
    lanes = 2 * side
    tiles = side // 2
    lower = lax.broadcasted_iota(jnp.int32, (tiles, lanes), 1) < side

    basis_in = basis_in_ref[...]
    in_high, in_low = split(twice_diagonal(basis_in))
    back_high, back_low = split(twice_diagonal(basis_in.T))
    ordered = jnp.concatenate(
        [basis_out_ref[pl.ds(0, tiles, stride=2), :], basis_out_ref[pl.ds(1, tiles, stride=2), :]], 0
    )
    out_high, out_low = split(ordered)
    turn_high, turn_low = split(ordered.T)
    inverse = 1.0 / (eigen_ref[...] + 0.1)
    inverse = jnp.concatenate([inverse, inverse], 1)

    stacked = jnp.concatenate(
        [q_ref[:, t * lanes:(t + 1) * lanes] for t in range(tiles)], 0
    )
    both = dot(stacked, jnp.concatenate([in_high, in_low], 1))
    rows_ref[...] = both[:, :lanes] + both[:, lanes:]

    pairs = []
    for pair in range(count // 2):
        first = rows_ref[pl.ds(2 * pair, tiles, stride=count), :]
        second = rows_ref[pl.ds(2 * pair + 1, tiles, stride=count), :]
        even = jnp.where(lower, first, swap_halves(second, side))
        odd = jnp.where(lower, swap_halves(first, side), second)
        pairs.append(jnp.concatenate([even, odd], 0))
    high, low = split(jnp.concatenate(pairs, 1))
    rotated = dot(
        jnp.concatenate([turn_high, turn_high, turn_low], 1), jnp.concatenate([high, low, high], 0)
    )
    scaled = rotated * jnp.concatenate([inverse] * (count // 2), 1)
    high, low = split(scaled)
    lifted = dot(
        jnp.concatenate([out_high, out_high, out_low], 1), jnp.concatenate([high, low, high], 0)
    )
    queries = []
    for pair in range(count // 2):
        even = lifted[:tiles, pair * lanes:(pair + 1) * lanes]
        odd = lifted[tiles:, pair * lanes:(pair + 1) * lanes]
        queries.append(jnp.where(lower, even, swap_halves(odd, side)))
        queries.append(jnp.where(lower, swap_halves(even, side), odd))
    high, low = split(jnp.concatenate(queries, 0))
    both = dot(
        jnp.concatenate([high, low], 1),
        jnp.concatenate(
            [
                jnp.concatenate([back_high, back_low], 1),
                jnp.concatenate([back_high, jnp.zeros_like(back_low)], 1),
            ],
            0,
        ),
    )
    rows_ref[...] = both[:, :lanes] + both[:, lanes:]
    for t in range(tiles):
        store(t, rows_ref[pl.ds(t, count, stride=tiles), :].astype(jnp.bfloat16))


def kernel(depth, pieces, q_hbm, basis_in_hbm, basis_out_hbm, eigen_hbm, t_hbm, o_ref,
           queries, basis_in, basis_out, eigen, rows, buf, train, own, outgoing, incoming,
           load_sem, recv, recv_core, send_right, send_left, send_y, send_core, recv_x, send_x):
    me = lax.axis_index("shard")
    layer = lax.axis_index("layer")
    core = lax.rem(me, 2)
    y = lax.rem(me // 2, 2)
    z = me // 4
    half = depth // 2
    mine = y * 2 + core
    across = (1 - y) * 2 + core
    sibling = y * 2 + (1 - core)
    diagonal = (1 - y) * 2 + (1 - core)

    smalls = [
        pltpu.make_async_copy(source, target, load_sem.at[index])
        for index, (source, target) in enumerate(
            [(q_hbm, queries), (basis_in_hbm, basis_in), (basis_out_hbm, basis_out), (eigen_hbm, eigen)]
        )
    ]
    for small in smalls:
        small.start()
    load = pltpu.make_async_copy(t_hbm, train, load_sem.at[len(smalls)])
    load.start()

    barrier = pltpu.get_barrier_semaphore()
    pl.semaphore_signal(barrier, inc=1, device_id={"shard": z * 4 + across}, device_id_type=MESH)
    pl.semaphore_signal(barrier, inc=1, device_id={"shard": z * 4 + sibling}, device_id_type=MESH)
    pl.semaphore_signal(barrier, inc=1, device_id={"layer": 1 - layer}, device_id_type=MESH)

    @pl.when(z > 0)
    def _():
        pl.semaphore_signal(barrier, inc=1, device_id={"shard": me - 4}, device_id_type=MESH)

    @pl.when(z < depth - 1)
    def _():
        pl.semaphore_signal(barrier, inc=1, device_id={"shard": me + 4}, device_id_type=MESH)

    for small in smalls:
        small.wait()

    def store(tile, value):
        per = buf.shape[-1] // value.shape[1]
        at = tile % per * value.shape[1]
        buf[z, mine, tile // per, :, at:at + value.shape[1]] = value

    precondition_block(queries, basis_in, basis_out, eigen, rows, store)
    pl.semaphore_wait(barrier, 3 + jnp.where(z > 0, 1, 0) + jnp.where(z < depth - 1, 1, 0))

    def chunk(column, row, piece, device, sem):
        return pltpu.make_async_remote_copy(
            src_ref=buf.at[column, row, piece],
            dst_ref=buf.at[column, row, piece],
            send_sem=sem,
            recv_sem=recv.at[column, row, piece],
            device_id={"shard": device},
            device_id_type=MESH,
        )

    def to_right(column, piece):
        return chunk(column, mine, piece, me + 4, send_right.at[column])

    def to_left(column, piece):
        return chunk(column, mine, piece, me - 4, send_left.at[column])

    def to_y(column, piece):
        return chunk(column, mine, piece, z * 4 + across, send_y.at[0])

    def to_core(column, row):
        return pltpu.make_async_remote_copy(
            src_ref=buf.at[column, row],
            dst_ref=buf.at[column, row],
            send_sem=send_core.at[0],
            recv_sem=recv_core.at[column, row],
            device_id={"shard": z * 4 + sibling},
            device_id_type=MESH,
        )

    def arrived(column, row, piece):
        chunk(column, row, piece, z * 4 + across, send_y.at[0]).wait_recv()

    def sent(region, sem):
        pltpu.make_async_copy(region, region, sem).wait()

    def partial_copy(slot):
        return pltpu.make_async_remote_copy(
            src_ref=outgoing.at[slot],
            dst_ref=incoming.at[slot],
            send_sem=send_x.at[slot],
            recv_sem=recv_x.at[slot],
            device_id={"layer": 1 - layer},
            device_id_type=MESH,
        )

    def along(column, piece):
        @pl.when(jnp.logical_and(column <= z, z < depth - 1))
        def _():
            to_right(column, piece).start()

        @pl.when(jnp.logical_and(column >= z, z > 0))
        def _():
            to_left(column, piece).start()

        to_y(column, piece).start()
        if piece == pieces - 1:
            to_core(column, mine).start()

    def from_row(column, piece):
        arrived(column, mine, piece)
        along(column, piece)

    def from_across(column, piece):
        arrived(column, across, piece)
        if piece == pieces - 1:
            to_core(column, across).start()

    def multiply(column):
        block = None
        to_core(column, sibling).wait_recv()
        to_core(column, diagonal).wait_recv()
        for piece in range(pieces):
            depth_of = buf.shape[-1]
            term = score_block(
                buf[column, :, piece].reshape(-1, depth_of),
                train[:, piece * depth_of:(piece + 1) * depth_of],
            )
            block = term if block is None else block + term
        slot = lax.rem(column, half)
        kept = column // half == layer

        @pl.when(kept)
        def _():
            own[slot] = block

        @pl.when(jnp.logical_not(kept))
        def _():
            outgoing[slot] = block.astype(outgoing.dtype)
            partial_copy(slot).start()

    def at_distance(step, act):
        if step == 0:
            act(z)
            return

        @pl.when(z >= step)
        def _():
            act(z - step)

        @pl.when(z + step < depth)
        def _():
            act(z + step)

    for piece in range(pieces):
        along(z, piece)
    for step in range(1, depth):
        for piece in range(pieces):
            at_distance(step, functools.partial(from_row, piece=piece))
            at_distance(step - 1, functools.partial(from_across, piece=piece))
        if step == 2:
            load.wait()
        if step >= 2:
            at_distance(step - 2, multiply)
    at_distance(depth - 2, multiply)
    for piece in range(pieces):
        at_distance(depth - 1, functools.partial(from_across, piece=piece))
    at_distance(depth - 1, multiply)

    sent(buf.at[:, mine], send_y.at[0])
    sent(buf.at[:, pl.ds(0, 2)], send_core.at[0])
    for column in range(depth):
        @pl.when(jnp.logical_and(z >= column, z < depth - 1))
        def _():
            sent(buf.at[column, mine], send_right.at[column])

        @pl.when(jnp.logical_and(z <= column, z > 0))
        def _():
            sent(buf.at[column, mine], send_left.at[column])

    for slot in range(half):
        partial_copy(slot).wait_recv()
        total = own[slot] + incoming[slot].astype(jnp.float32)
        own[slot] = total
    o_ref[...] = own[...].reshape(-1, own.shape[-1]).T

    for slot in range(half):
        partial_copy(slot).wait_send()


def fused_scores(queries, basis_in, basis_out, eigen, train_flat, shards):
    count, width = queries.shape
    side = basis_in.shape[-1]
    examples = train_flat.shape[0]
    depth = shards // 4
    half = depth // 2
    pieces = PIECES
    dma = pltpu.SemaphoreType.DMA
    return pl.pallas_call(
        functools.partial(kernel, depth, pieces),
        out_shape=jax.ShapeDtypeStruct((examples, half * 4 * count), jnp.float32),
        in_specs=[pl.BlockSpec(memory_space=pl.ANY)] * 5,
        out_specs=pl.BlockSpec(memory_space=pltpu.VMEM),
        scratch_shapes=[
            pltpu.VMEM((count, width), jnp.bfloat16),
            pltpu.VMEM((side, side), jnp.float32),
            pltpu.VMEM((side, side), jnp.float32),
            pltpu.VMEM((side, side), jnp.float32),
            pltpu.VMEM((count * side // 2, 2 * side), jnp.float32),
            pltpu.VMEM((depth, 4, pieces, count, width // pieces), jnp.bfloat16),
            pltpu.VMEM((examples, width), jnp.bfloat16),
            pltpu.VMEM((half, 4 * count, examples), jnp.float32),
            pltpu.VMEM((half, 4 * count, examples), jnp.bfloat16),
            pltpu.VMEM((half, 4 * count, examples), jnp.bfloat16),
            dma((5,)),
            dma((depth, 4, pieces)),
            dma((depth, 4)),
            dma((depth,)),
            dma((depth,)),
            dma((1,)),
            dma((1,)),
            dma((half,)),
            dma((half,)),
        ],
        compiler_params=pltpu.CompilerParams(
            collective_id=0, has_side_effects=True, vmem_limit_bytes=60 * 1024 * 1024
        ),
    )(queries, basis_in, basis_out, eigen, train_flat)


def body(fused, shards, train_grads, queries, basis_in, basis_out, eigen):
    examples = train_grads.shape[0]
    train_flat = train_grads.reshape(examples, train_grads.shape[1] * train_grads.shape[2])
    if fused:
        return fused_scores(
            queries.reshape(queries.shape[0], -1), basis_in[0], basis_out[0], eigen[0], train_flat, shards
        )
    precond = precondition(queries, basis_in, basis_out, eigen)
    gathered = lax.all_gather(precond, "shard", axis=0, tiled=True)
    mine = lax.psum_scatter(
        score_block(gathered, train_flat), "layer", scatter_dimension=0, tiled=True
    )
    return jnp.transpose(mine)


def solution(mesh):
    placed = (
        P(("groups", "shard"), "layer", None),
        P("shard", "layer", None),
        P("layer", None, None),
        P("layer", None, None),
        P("layer", None, None),
    )
    shards = mesh.shape["shard"]
    fused = mesh.shape["groups"] == 1 and mesh.shape["layer"] == 2 and shards == 16
    return jax.shard_map(
        functools.partial(body, fused, shards), mesh=mesh, in_specs=placed,
        out_specs=P(("groups", "shard"), "layer"), check_vma=False
    )
```

```python
import functools

import jax
import jax.numpy as jnp
from jax import lax
from jax.experimental import pallas as pl
from jax.experimental.pallas import tpu as pltpu
from jax.sharding import PartitionSpec as P

MESH = pl.DeviceIdType.MESH
PIECES = 2


def precondition(queries, basis_in, basis_out, eigen):
    count = queries.shape[0]
    layers = queries.shape[1]
    side = basis_in.shape[-1]
    grads = queries.astype(jnp.float32).reshape(count, layers, side, side)
    highest = lax.Precision.HIGHEST
    rotated = jnp.einsum("lai,qlab,lbj->qlij", basis_out, grads, basis_in, precision=highest)
    scaled = rotated / (eigen + 0.1)
    result = jnp.einsum("lia,qlab,ljb->qlij", basis_out, scaled, basis_in, precision=highest)
    return result.reshape(count, layers * side * side).astype(jnp.bfloat16)


def score_block(left, right):
    return lax.dot_general(
        left, right, (((1,), (1,)), ((), ())), preferred_element_type=jnp.float32
    )


def split(value):
    high = value.astype(jnp.bfloat16)
    return high, (value - high.astype(jnp.float32)).astype(jnp.bfloat16)


def dot(left, right):
    return jnp.dot(left, right, preferred_element_type=jnp.float32)


def twice_diagonal(block):
    empty = jnp.zeros_like(block)
    return jnp.concatenate(
        [jnp.concatenate([block, empty], 1), jnp.concatenate([empty, block], 1)], 0
    )


def swap_halves(value, side):
    return pltpu.roll(value, side, 1)


def precondition_block(q_ref, basis_in_ref, basis_out_ref, eigen_ref, rows_ref, store):
    count = q_ref.shape[0]
    side = basis_in_ref.shape[-1]
    lanes = 2 * side
    tiles = side // 2
    lower = lax.broadcasted_iota(jnp.int32, (tiles, lanes), 1) < side

    basis_in = basis_in_ref[...]
    in_high, in_low = split(twice_diagonal(basis_in))
    back_high, back_low = split(twice_diagonal(basis_in.T))
    ordered = jnp.concatenate(
        [basis_out_ref[pl.ds(0, tiles, stride=2), :], basis_out_ref[pl.ds(1, tiles, stride=2), :]], 0
    )
    out_high, out_low = split(ordered)
    turn_high, turn_low = split(ordered.T)
    inverse = 1.0 / (eigen_ref[...] + 0.1)
    inverse = jnp.concatenate([inverse, inverse], 1)

    stacked = jnp.concatenate(
        [q_ref[:, t * lanes:(t + 1) * lanes] for t in range(tiles)], 0
    )
    both = dot(stacked, jnp.concatenate([in_high, in_low], 1))
    rows_ref[...] = both[:, :lanes] + both[:, lanes:]

    pairs = []
    for pair in range(count // 2):
        first = rows_ref[pl.ds(2 * pair, tiles, stride=count), :]
        second = rows_ref[pl.ds(2 * pair + 1, tiles, stride=count), :]
        even = jnp.where(lower, first, swap_halves(second, side))
        odd = jnp.where(lower, swap_halves(first, side), second)
        pairs.append(jnp.concatenate([even, odd], 0))
    high, low = split(jnp.concatenate(pairs, 1))
    rotated = dot(
        jnp.concatenate([turn_high, turn_high, turn_low], 1), jnp.concatenate([high, low, high], 0)
    )
    scaled = rotated * jnp.concatenate([inverse] * (count // 2), 1)
    high, low = split(scaled)
    lifted = dot(
        jnp.concatenate([out_high, out_high, out_low], 1), jnp.concatenate([high, low, high], 0)
    )
    queries = []
    for pair in range(count // 2):
        even = lifted[:tiles, pair * lanes:(pair + 1) * lanes]
        odd = lifted[tiles:, pair * lanes:(pair + 1) * lanes]
        queries.append(jnp.where(lower, even, swap_halves(odd, side)))
        queries.append(jnp.where(lower, swap_halves(even, side), odd))
    high, low = split(jnp.concatenate(queries, 0))
    both = dot(
        jnp.concatenate([high, low], 1),
        jnp.concatenate(
            [
                jnp.concatenate([back_high, back_low], 1),
                jnp.concatenate([back_high, jnp.zeros_like(back_low)], 1),
            ],
            0,
        ),
    )
    rows_ref[...] = both[:, :lanes] + both[:, lanes:]
    for t in range(tiles):
        store(t, rows_ref[pl.ds(t, count, stride=tiles), :].astype(jnp.bfloat16))


def kernel(depth, pieces, q_hbm, basis_in_hbm, basis_out_hbm, eigen_hbm, t_hbm, o_ref,
           queries, basis_in, basis_out, eigen, rows, buf, train, own, outgoing, incoming,
           load_sem, recv, recv_core, send_right, send_left, send_y, send_core, recv_x, send_x):
    me = lax.axis_index("shard")
    layer = lax.axis_index("layer")
    core = lax.rem(me, 2)
    y = lax.rem(me // 2, 2)
    z = me // 4
    half = depth // 2
    mine = y * 2 + core
    across = (1 - y) * 2 + core
    sibling = y * 2 + (1 - core)
    diagonal = (1 - y) * 2 + (1 - core)

    smalls = [
        pltpu.make_async_copy(source, target, load_sem.at[index])
        for index, (source, target) in enumerate(
            [(q_hbm, queries), (basis_in_hbm, basis_in), (basis_out_hbm, basis_out), (eigen_hbm, eigen)]
        )
    ]
    for small in smalls:
        small.start()
    load = pltpu.make_async_copy(t_hbm, train, load_sem.at[len(smalls)])
    load.start()

    barrier = pltpu.get_barrier_semaphore()
    pl.semaphore_signal(barrier, inc=1, device_id={"shard": z * 4 + across}, device_id_type=MESH)
    pl.semaphore_signal(barrier, inc=1, device_id={"shard": z * 4 + sibling}, device_id_type=MESH)
    pl.semaphore_signal(barrier, inc=1, device_id={"layer": 1 - layer}, device_id_type=MESH)

    @pl.when(z > 0)
    def _():
        pl.semaphore_signal(barrier, inc=1, device_id={"shard": me - 4}, device_id_type=MESH)

    @pl.when(z < depth - 1)
    def _():
        pl.semaphore_signal(barrier, inc=1, device_id={"shard": me + 4}, device_id_type=MESH)

    for small in smalls:
        small.wait()

    def store(tile, value):
        per = buf.shape[-1] // value.shape[1]
        at = tile % per * value.shape[1]
        buf[z, mine, tile // per, :, at:at + value.shape[1]] = value

    precondition_block(queries, basis_in, basis_out, eigen, rows, store)
    pl.semaphore_wait(barrier, 3 + jnp.where(z > 0, 1, 0) + jnp.where(z < depth - 1, 1, 0))

    def chunk(column, row, piece, device, sem):
        return pltpu.make_async_remote_copy(
            src_ref=buf.at[column, row, piece],
            dst_ref=buf.at[column, row, piece],
            send_sem=sem,
            recv_sem=recv.at[column, row, piece],
            device_id={"shard": device},
            device_id_type=MESH,
        )

    def to_right(column, piece):
        return chunk(column, mine, piece, me + 4, send_right.at[column])

    def to_left(column, piece):
        return chunk(column, mine, piece, me - 4, send_left.at[column])

    def to_y(column, piece):
        return chunk(column, mine, piece, z * 4 + across, send_y.at[0])

    def to_core(column, row):
        return pltpu.make_async_remote_copy(
            src_ref=buf.at[column, row],
            dst_ref=buf.at[column, row],
            send_sem=send_core.at[0],
            recv_sem=recv_core.at[column, row],
            device_id={"shard": z * 4 + sibling},
            device_id_type=MESH,
        )

    def arrived(column, row, piece):
        chunk(column, row, piece, z * 4 + across, send_y.at[0]).wait_recv()

    def sent(region, sem):
        pltpu.make_async_copy(region, region, sem).wait()

    def partial_copy(slot):
        return pltpu.make_async_remote_copy(
            src_ref=outgoing.at[slot],
            dst_ref=incoming.at[slot],
            send_sem=send_x.at[slot],
            recv_sem=recv_x.at[slot],
            device_id={"layer": 1 - layer},
            device_id_type=MESH,
        )

    def along(column, piece):
        @pl.when(jnp.logical_and(column <= z, z < depth - 1))
        def _():
            to_right(column, piece).start()

        @pl.when(jnp.logical_and(column >= z, z > 0))
        def _():
            to_left(column, piece).start()

        to_y(column, piece).start()
        if piece == pieces - 1:
            to_core(column, mine).start()

    def from_row(column, piece):
        arrived(column, mine, piece)
        along(column, piece)

    def from_across(column, piece):
        arrived(column, across, piece)
        if piece == pieces - 1:
            to_core(column, across).start()

    def multiply(column):
        block = None
        to_core(column, sibling).wait_recv()
        to_core(column, diagonal).wait_recv()
        for piece in range(pieces):
            depth_of = buf.shape[-1]
            term = score_block(
                train[:, piece * depth_of:(piece + 1) * depth_of],
                buf[column, :, piece].reshape(-1, depth_of),
            )
            block = term if block is None else block + term
        block = block.T
        slot = lax.rem(column, half)
        kept = column // half == layer

        @pl.when(kept)
        def _():
            own[slot] = block

        @pl.when(jnp.logical_not(kept))
        def _():
            outgoing[slot] = block.astype(outgoing.dtype)
            partial_copy(slot).start()

    def at_distance(step, act):
        if step == 0:
            act(z)
            return

        @pl.when(z >= step)
        def _():
            act(z - step)

        @pl.when(z + step < depth)
        def _():
            act(z + step)

    for piece in range(pieces):
        along(z, piece)
    for step in range(1, depth):
        for piece in range(pieces):
            at_distance(step, functools.partial(from_row, piece=piece))
            at_distance(step - 1, functools.partial(from_across, piece=piece))
        if step == 2:
            load.wait()
        if step >= 2:
            at_distance(step - 2, multiply)
    at_distance(depth - 2, multiply)
    for piece in range(pieces):
        at_distance(depth - 1, functools.partial(from_across, piece=piece))
    at_distance(depth - 1, multiply)

    sent(buf.at[:, mine], send_y.at[0])
    sent(buf.at[:, pl.ds(0, 2)], send_core.at[0])
    for column in range(depth):
        @pl.when(jnp.logical_and(z >= column, z < depth - 1))
        def _():
            sent(buf.at[column, mine], send_right.at[column])

        @pl.when(jnp.logical_and(z <= column, z > 0))
        def _():
            sent(buf.at[column, mine], send_left.at[column])

    for slot in range(half):
        partial_copy(slot).wait_recv()
        total = own[slot] + incoming[slot].astype(jnp.float32)
        own[slot] = total
    o_ref[...] = own[...].reshape(-1, own.shape[-1]).T

    for slot in range(half):
        partial_copy(slot).wait_send()


def fused_scores(queries, basis_in, basis_out, eigen, train_flat, shards):
    count, width = queries.shape
    side = basis_in.shape[-1]
    examples = train_flat.shape[0]
    depth = shards // 4
    half = depth // 2
    pieces = PIECES
    dma = pltpu.SemaphoreType.DMA
    return pl.pallas_call(
        functools.partial(kernel, depth, pieces),
        out_shape=jax.ShapeDtypeStruct((examples, half * 4 * count), jnp.float32),
        in_specs=[pl.BlockSpec(memory_space=pl.ANY)] * 5,
        out_specs=pl.BlockSpec(memory_space=pltpu.VMEM),
        scratch_shapes=[
            pltpu.VMEM((count, width), jnp.bfloat16),
            pltpu.VMEM((side, side), jnp.float32),
            pltpu.VMEM((side, side), jnp.float32),
            pltpu.VMEM((side, side), jnp.float32),
            pltpu.VMEM((count * side // 2, 2 * side), jnp.float32),
            pltpu.VMEM((depth, 4, pieces, count, width // pieces), jnp.bfloat16),
            pltpu.VMEM((examples, width), jnp.bfloat16),
            pltpu.VMEM((half, 4 * count, examples), jnp.float32),
            pltpu.VMEM((half, 4 * count, examples), jnp.bfloat16),
            pltpu.VMEM((half, 4 * count, examples), jnp.bfloat16),
            dma((5,)),
            dma((depth, 4, pieces)),
            dma((depth, 4)),
            dma((depth,)),
            dma((depth,)),
            dma((1,)),
            dma((1,)),
            dma((half,)),
            dma((half,)),
        ],
        compiler_params=pltpu.CompilerParams(
            collective_id=0, has_side_effects=True, vmem_limit_bytes=60 * 1024 * 1024
        ),
    )(queries, basis_in, basis_out, eigen, train_flat)


def body(fused, shards, train_grads, queries, basis_in, basis_out, eigen):
    examples = train_grads.shape[0]
    train_flat = train_grads.reshape(examples, train_grads.shape[1] * train_grads.shape[2])
    if fused:
        return fused_scores(
            queries.reshape(queries.shape[0], -1), basis_in[0], basis_out[0], eigen[0], train_flat, shards
        )
    precond = precondition(queries, basis_in, basis_out, eigen)
    gathered = lax.all_gather(precond, "shard", axis=0, tiled=True)
    mine = lax.psum_scatter(
        score_block(gathered, train_flat), "layer", scatter_dimension=0, tiled=True
    )
    return jnp.transpose(mine)


def solution(mesh):
    placed = (
        P(("groups", "shard"), "layer", None),
        P("shard", "layer", None),
        P("layer", None, None),
        P("layer", None, None),
        P("layer", None, None),
    )
    shards = mesh.shape["shard"]
    fused = mesh.shape["groups"] == 1 and mesh.shape["layer"] == 2 and shards == 16
    return jax.shard_map(
        functools.partial(body, fused, shards), mesh=mesh, in_specs=placed,
        out_specs=P(("groups", "shard"), "layer"), check_vma=False
    )
```
